256 devices in a mesh: expert: 64 (over z_lo, y, x, core), helper: 4 (over z_hi).
Axes of the slice: x: 4, y: 4, z: 8 (z_hi: 4, z_lo: 2; z = z_hi * 2 + z_lo), core: 2. Of those that a mesh axis runs over, the one named last changes fastest.
Arguments:
- tokens: bfloat16 [8192, 2048], P(('expert', 'helper')), may hold values from -20 to 20, as said below
- routes: int32 [8192, 8], P(('expert', 'helper')), may hold values from 0 to 127, all different within a row; in each aligned block of 32 rows (0 to 31, 32 to 63, ...) at most 4 rows name the same one
- chosen: int32 [64], replicated, may hold values from 0 to 127, as said below
Outputs:
- hessian: float32 [64, 2048, 2048], P('expert', 'helper')
- inverse: bfloat16 [64, 2048, 2048], P('expert', None, 'helper')
The draws below stay inside these ranges and needn't reach their ends.
Inputs may be any that keep to these rules, and one draw needn't show every extreme that they name: `routes`: within the 32 rows of one device, no expert is named by more than 4 rows, a bound that some block reaches; every expert is named by some token. `chosen`: the 64 entries are distinct. `tokens`: no row is entirely zero.
All inputs are finite; a program needn't handle non-finite values.
Results may differ from the reference program's by a relative error of at most 0.0025.
Values may be sent and summed in bfloat16 or wider, within the bound.
No kernel may reach another device: no remote copies, remote signals or barrier semaphores. Data moves between devices by JAX's collectives and lax.ppermute only.
A program may use at most 128 MiB of HBM per device.

```python
import math
import jax
import jax.numpy as jnp
import numpy as np
from jax import lax

D = 2048
EXPERTS = 128
TOP = 8
TOK_DEV = 32
MOST = 4
SLOTS = 64
TOKENS = 8192
CAP_ALL = 1024


def draw_tokens(key, part):
    key = jax.random.fold_in(key, 3)
    key_row, key_col, key_base = jax.random.split(key, 3)
    row_scale = jnp.exp(jax.random.uniform(key_row, (TOKENS, 1), minval=-0.8, maxval=0.8))
    col_scale = jnp.exp(jax.random.uniform(key_col, (1, D), minval=-0.8, maxval=0.8))
    base = jnp.clip(jax.random.normal(key_base, (TOKENS, D)), -4.0, 4.0)
    return (base * row_scale * col_scale).astype(jnp.bfloat16)


def draw_chosen(key, part):
    key = jax.random.fold_in(key, 7)
    return jax.random.permutation(key, EXPERTS)[:SLOTS].astype(jnp.int32)


def routed_block(stream_key, own, number, rows, number_of, top, most, skew):
    sequence = jax.random.permutation(stream_key, number_of)
    packed, usual = portions_of(number_of, rows * top, most, skew, True), portions_of(number_of, rows * top, most, skew, False)
    places = jnp.arange(number_of)

    def named(sizes, rotation):
        used = int((sizes > 0).sum())
        fixed = max(1, used // 4)
        moved = fixed + (places - fixed + rotation * (used - fixed)) % max(1, number_of - fixed)
        return jnp.zeros((number_of,), jnp.int32).at[sequence[jnp.where(places < fixed, places, moved)]].set(jnp.asarray(sizes, jnp.int32))

    sizes = jnp.where(number % 4 == 0, named(packed, number // 4), named(usual, number - number // 4 - 1))
    mixed = jax.random.permutation(jax.random.fold_in(own, 3), number_of)
    donor, sink = mixed[0:number_of // 2 * 2:2], mixed[1:number_of // 2 * 2:2]
    margin = jnp.minimum(sizes[donor] - 1, most - sizes[sink]) // 2
    margin = jnp.where((donor == sequence[0]) | (sink == sequence[0]) | (sizes[sink] == 0), 0, jnp.maximum(margin, 0))
    moved = jax.random.randint(jax.random.fold_in(own, 4), (number_of // 2,), 0, 1 << 20) % (margin + 1)
    sizes = sizes.at[donor].add(-moved).at[sink].add(moved)
    items = jnp.searchsorted(jnp.cumsum(sizes), jnp.arange(rows * top), side="right").astype(jnp.int32)
    table = items.reshape(top, rows).T
    table = table[jax.random.permutation(jax.random.fold_in(own, 1), rows)]
    rotation = jax.random.randint(jax.random.fold_in(own, 2), (rows, 1), 0, top)
    return jnp.take_along_axis(table, (jnp.arange(top)[None, :] + rotation) % top, axis=1)


def portions_of(number_of, total, reach, slope, full):
    loads = [(1 << 20) // math.isqrt(grade ** slope) + 1 for grade in range(1, number_of + 1)]
    largest = reach if full else min(reach, max(-(-total // number_of), total * loads[0] // sum(loads)))
    least = 1 if total - largest >= number_of - 1 else 0
    counts, spare = [largest] + [least] * (number_of - 1), total - largest - least * (number_of - 1)
    while spare > 0:
        free = [i for i in range(1, number_of) if counts[i] < largest] or [i for i in range(1, number_of) if counts[i] < reach]
        whole, left = sum([loads[i] for i in free]), spare
        for i in free:
            addition = min(reach - counts[i], max(1, left * loads[i] // whole), spare)
            counts[i] = counts[i] + addition
            spare = spare - addition
    return np.array(counts)


def setup_inputs(seed: int = 0) -> dict:
    key_list = jax.random.split(jax.random.key(seed), 4)
    tokens = draw_tokens(jax.random.fold_in(key_list[3], 71), 0)
    routes_keys = jax.random.split(jax.random.fold_in(key_list[1], 1), TOKENS // TOK_DEV)
    routes_turns = jax.random.permutation(jax.random.fold_in(key_list[1], 3), TOKENS // TOK_DEV)
    routes = jax.vmap(lambda own, number: routed_block(jax.random.fold_in(key_list[1], 2), own, number, TOK_DEV, EXPERTS, TOP, MOST, 2))(routes_keys, routes_turns).reshape((TOKENS, TOP))
    chosen = draw_chosen(jax.random.fold_in(key_list[3], 71), 0)
    return {"tokens": tokens, "routes": routes, "chosen": chosen}


def reference(tokens, routes, chosen):
    data = tokens.astype(jnp.float32)
    eye = jnp.eye(D, dtype=jnp.float32)

    def one_expert(expert):
        named = jnp.sum((routes == expert).astype(jnp.int32), axis=1)
        count = jnp.sum(named)
        order = jnp.nonzero(named, size=CAP_ALL, fill_value=0)[0].astype(jnp.int32)
        keep = (jnp.arange(CAP_ALL, dtype=jnp.int32) < count).astype(jnp.float32)
        picked = data[order] * keep[:, None]
        gram = lax.dot_general(picked, picked, (((0,), (0,)), ((), ())), precision=lax.Precision.HIGHEST)
        scale = 2.0 / count.astype(jnp.float32)
        damp = 0.01 * scale * jnp.trace(gram) / D
        hessian = gram * scale + damp * eye
        factor = jnp.linalg.cholesky(hessian)
        solved = lax.linalg.triangular_solve(factor, eye, left_side=True, lower=True)
        return (hessian, solved.astype(jnp.bfloat16))
    hessian, inverse = lax.map(one_expert, chosen)
    return (hessian, inverse)
```

```python
import functools

import jax
import jax.numpy as jnp
from jax import lax
from jax.experimental import pallas as pl
from jax.experimental.pallas import tpu as pltpu
from jax.sharding import PartitionSpec as P

MOST = 4
BLOCK = 128
TILE = 256
CHAIN = 8

f32 = jnp.float32
bf16 = jnp.bfloat16


def at(index, size):
    return pl.ds(pl.multiple_of(index * size, size), size)


def multiply(left, right):
    return jnp.dot(left, right, preferred_element_type=f32)


def pieces(value):
    high = value.astype(bf16)
    rest = value - high.astype(f32)
    middle = rest.astype(bf16)
    return high, middle, (rest - middle.astype(f32)).astype(bf16)


def as_left(value):
    high, middle, low = pieces(value)
    return jnp.concatenate([high, high, middle, middle, high, low], axis=1)


def as_right(value):
    high, middle, low = pieces(value)
    return jnp.concatenate([high, middle, high, middle, low, high], axis=0)


def spread_row(group, row):
    return jnp.broadcast_to(group[row : row + 1, :], group.shape)


def spread_lane(group, lane):
    return jnp.broadcast_to(group[:, lane : lane + 1], group.shape)


def inverse_factor(groups):
    number = len(groups)
    groups = list(groups)
    row = lax.broadcasted_iota(jnp.int32, (8, BLOCK), 0)
    lane = lax.broadcasted_iota(jnp.int32, (8, BLOCK), 1)
    result = []
    for first in range(number):
        columns = [
            [spread_lane(groups[g], CHAIN * first + k) for g in range(first, number)]
            for k in range(CHAIN)
        ]
        norms = []
        for j in range(CHAIN):
            pivot = spread_row(columns[j][0], j)
            scale = 1.0 / pivot
            norms.append(lax.rsqrt(pivot))
            hit = lane == CHAIN * first + j
            pivot_row = jnp.where(hit, 1.0, spread_row(groups[first], j))
            heads = [spread_row(columns[k][0], j) for k in range(j + 1, CHAIN)]
            for g in range(first, number):
                factor = columns[j][g - first] * scale
                below = hit
                if g == first:
                    factor = jnp.where(row > j, factor, 0.0)
                    below = hit & (row > j)
                groups[g] = jnp.where(below, 0.0, groups[g]) - factor * pivot_row
                for k in range(j + 1, CHAIN):
                    columns[k][g - first] -= factor * heads[k - j - 1]
        norm = norms[0]
        for j in range(1, CHAIN):
            norm = jnp.where(row == j, norms[j], norm)
        diagonal = row + CHAIN * first
        unit = jnp.where(lane < diagonal, groups[first], 0.0)
        result.append(jnp.where(lane == diagonal, 1.0, unit) * norm)
    return jnp.concatenate(result, axis=0)


def kernel(here_ref, rows_ref, hessian_ref, inverse_ref, work, upper, lower, turned):
    here = here_ref[0]
    count_rows, width = rows_ref.shape
    share = hessian_ref.shape[0]
    tiles = width // TILE
    share_tiles = share // TILE

    def add_up(i, sums):
        squares, live = sums
        part = rows_ref[at(i, 32), :].astype(f32)
        squares = squares + jnp.sum((part * part).reshape(4, 8, width), axis=0)
        named = jnp.max(jnp.abs(part), axis=1, keepdims=True) > 0.0
        return squares, live + named.astype(f32)

    squares, live = lax.fori_loop(
        0, count_rows // 32, add_up, (jnp.zeros((8, width), f32), jnp.zeros((32, 1), f32))
    )
    scale = 2.0 / jnp.sum(live, axis=0, keepdims=True)
    trace = jnp.sum(jnp.sum(squares, axis=1, keepdims=True), axis=0, keepdims=True)
    damp = 0.01 * scale * trace / width

    def diagonal(first_row, first_column):
        row = lax.broadcasted_iota(jnp.int32, (TILE, TILE), 0) + first_row
        return row == lax.broadcasted_iota(jnp.int32, (TILE, TILE), 1) + first_column

    def hessian_tile(t, first_row):
        gram = multiply(turned[...], rows_ref[:, at(t, TILE)])
        return gram * scale + jnp.where(diagonal(first_row, t * TILE), damp, 0.0)

    def fill(i, carry):
        turned[...] = rows_ref[:, at(i, TILE)].T

        def tile(t, carry):
            work[at(i, TILE), at(t, TILE)] = hessian_tile(t, i * TILE)
            return carry

        lax.fori_loop(i, tiles, tile, 0)
        for t in range(share_tiles):
            unit = diagonal(i * TILE, here * share + t * TILE)
            work[at(i, TILE), pl.ds(width + t * TILE, TILE)] = unit.astype(f32)
        return carry

    lax.fori_loop(0, tiles, fill, 0)

    def own(i, carry):
        block = here * share_tiles + i
        turned[...] = rows_ref[:, at(block, TILE)].T

        def tile(t, carry):
            hessian_ref[at(i, TILE), at(t, TILE)] = hessian_tile(t, block * TILE)
            return carry

        return lax.fori_loop(0, tiles, tile, carry)

    lax.fori_loop(0, share_tiles, own, 0)

    def step(k, carry):
        groups = [
            work[pl.ds(pl.multiple_of(k * BLOCK + 8 * g, 8), 8), at(k, BLOCK)]
            for g in range(BLOCK // 8)
        ]
        solve = as_left(inverse_factor(groups))
        first = (k + 1) // 2

        def panel(t):
            solved = multiply(solve, as_right(work[at(k, BLOCK), at(t, TILE)]))
            upper[:, at(t, TILE)] = as_right(solved)
            return solved

        def factor_tile(t, carry):
            lower[at(t, TILE), :] = as_left(panel(t).T)
            return carry

        def inverse_tile(t, carry):
            inverse_ref[at(k, BLOCK), at(t - tiles, TILE)] = panel(t).astype(bf16)
            return carry

        lax.fori_loop(first, tiles, factor_tile, 0)
        lax.fori_loop(tiles, tiles + share_tiles, inverse_tile, 0)

        def trailing_row(i, carry):
            def tile(t, carry):
                spot = (at(i, TILE), at(t, TILE))
                work[spot] = work[spot] - multiply(lower[at(i, TILE), :], upper[:, at(t, TILE)])
                return carry

            return lax.fori_loop(i, tiles + share_tiles, tile, carry)

        return lax.fori_loop(first, tiles, trailing_row, carry)

    lax.fori_loop(0, width // BLOCK, step, 0)


def factor(here, rows, share):
    count_rows, width = rows.shape
    return pl.pallas_call(
        kernel,
        out_shape=(
            jax.ShapeDtypeStruct((share, width), f32),
            jax.ShapeDtypeStruct((width, share), bf16),
        ),
        in_specs=[
            pl.BlockSpec(memory_space=pltpu.SMEM),
            pl.BlockSpec(memory_space=pltpu.VMEM),
        ],
        out_specs=(pl.BlockSpec(memory_space=pltpu.VMEM),) * 2,
        scratch_shapes=[
            pltpu.VMEM((width, width + share), f32),
            pltpu.VMEM((6 * BLOCK, width + share), bf16),
            pltpu.VMEM((width, 6 * BLOCK), bf16),
            pltpu.VMEM((TILE, count_rows), bf16),
        ],
        compiler_params=pltpu.CompilerParams(vmem_limit_bytes=56 * 2**20),
        name="factor",
    )(here, rows)


def local(tokens, routes, chosen):
    slots = chosen.shape[0]
    width = tokens.shape[1]
    flat = routes.reshape(-1)
    hits = (flat[:, None] == chosen[None, :]).astype(jnp.int32)
    before = jnp.cumsum(hits, axis=0) - hits
    slot_base = jnp.arange(slots, dtype=jnp.int32)[None, :] * MOST
    target = jnp.sum(hits * (slot_base + before), axis=1)
    named = jnp.sum(hits, axis=1)
    places = jnp.arange(slots * MOST, dtype=jnp.int32)
    picks = ((places[:, None] == target[None, :]) & (named[None, :] > 0)).astype(jnp.bfloat16)
    picks = jnp.sum(picks.reshape(slots * MOST, routes.shape[0], routes.shape[1]), axis=2)
    outgoing = jnp.dot(picks, tokens, preferred_element_type=jnp.float32).astype(jnp.bfloat16)
    outgoing = outgoing.reshape(slots, MOST, width)
    arrived = lax.all_to_all(outgoing, "expert", split_axis=0, concat_axis=0, tiled=True).reshape(
        -1, width
    )
    rows = lax.all_gather(arrived, "helper", axis=0, tiled=True)
    here = lax.axis_index("helper").astype(jnp.int32).reshape(1)
    hessian, inverse = factor(here, rows, width // lax.axis_size("helper"))
    return (hessian[None], inverse[None])


def solution(mesh):
    placed = (P(("expert", "helper"), None), P(("expert", "helper"), None), P())
    return jax.shard_map(
        local,
        mesh=mesh,
        in_specs=placed,
        out_specs=(P("expert", "helper", None), P("expert", None, "helper")),
        check_vma=False,
    )
```

```python
import functools

import jax
import jax.numpy as jnp
from jax import lax
from jax.experimental import pallas as pl
from jax.experimental.pallas import tpu as pltpu
from jax.sharding import PartitionSpec as P

MOST = 4
BLOCK = 128
PANEL = 256
SHARE = 2
CHAIN = 8

f32 = jnp.float32
bf16 = jnp.bfloat16


def multiply(left, right):
    return jnp.dot(left, right, preferred_element_type=f32)


def pieces(value):
    high = value.astype(bf16)
    rest = value - high.astype(f32)
    middle = rest.astype(bf16)
    return high, middle, (rest - middle.astype(f32)).astype(bf16)


def left_of(parts):
    high, middle, low = parts
    return jnp.concatenate([high, high, middle, middle, high, low], axis=1)


def right_of(parts):
    high, middle, low = parts
    return jnp.concatenate([high, middle, high, middle, low, high], axis=0)


def product(left, right):
    return multiply(left_of(pieces(left)), right_of(pieces(right)))


def spread_row(group, row):
    return jnp.broadcast_to(group[row : row + 1, :], group.shape)


def spread_lane(group, lane):
    return jnp.broadcast_to(group[:, lane : lane + 1], group.shape)


def inverse_factor(groups):
    groups = list(groups)
    row = lax.broadcasted_iota(jnp.int32, (8, BLOCK), 0)
    lane = lax.broadcasted_iota(jnp.int32, (8, BLOCK), 1)
    below = [row > j for j in range(8)]
    result = []
    for first in range(len(groups)):
        base = 8 * first
        columns = [spread_lane(groups[first], base + k) for k in range(8)]
        scales, norms, heads, factors = [], [], [], []
        for j in range(8):
            pivot = spread_row(columns[j], j)
            scales.append(1.0 / pivot)
            norms.append(lax.rsqrt(pivot))
            heads.append([spread_row(columns[k], j) for k in range(j + 1, 8)])
            under = jnp.where(below[j], columns[j], 0.0)
            factors.append(under * scales[j])
            for k in range(j + 1, 8):
                columns[k] = columns[k] - (under * heads[j][k - j - 1]) * scales[j]
        pivot_rows = []
        own = groups[first]
        for j in range(8):
            hit = lane == base + j
            pivot_row = jnp.where(hit, 1.0, spread_row(own, j))
            pivot_rows.append(jnp.where((lane > base + j) & (lane < base + 8), 0.0, pivot_row))
            if j < 7:
                own = jnp.where(hit & below[j], 0.0, own) - factors[j] * pivot_row
        inside = (lane >= base) & (lane < base + 8)
        for g in range(first + 1, len(groups)):
            columns = [spread_lane(groups[g], base + k) for k in range(8)]
            rest = jnp.where(inside, 0.0, groups[g])
            for j in range(8):
                factor = columns[j] * scales[j]
                for k in range(j + 1, 8):
                    columns[k] = columns[k] - factor * heads[j][k - j - 1]
                rest = rest - factor * pivot_rows[j]
            groups[g] = rest
        norm = norms[0]
        for j in range(1, 8):
            norm = jnp.where(row == j, norms[j], norm)
        unit = jnp.where(lane < row + base, own, 0.0)
        result.append(jnp.where(lane == row + base, 1.0, unit) * norm)
    return jnp.concatenate(result, axis=0)


def diagonal(shape, offset):
    row = lax.broadcasted_iota(jnp.int32, shape, 0) + offset
    return row == lax.broadcasted_iota(jnp.int32, shape, 1)


def span(panel, number=1):
    return slice(panel * PANEL, (panel + number) * PANEL)


FIRST, SECOND = slice(0, BLOCK), slice(BLOCK, PANEL)


def panels_kernel(panels, total, inputs, outputs, scratch, here_ref, stats_ref, *refs):
    names = [*inputs, *outputs, *scratch]
    ref = dict(zip(names, refs))
    here = here_ref[0]
    scale, damp = stats_ref[0], stats_ref[1]
    top, bottom, across, between = (ref[n] for n in ("top", "bottom", "across", "between"))
    turned = ref["turned"]

    def work(panel):
        return ref["work", panel % 2]

    def lower(panel):
        return ref["lower", panel % 2]

    def load(name, panel, rows=slice(None), lanes=slice(None)):
        return [ref[name, panel][i, rows, lanes] for i in range(3)]

    def store(target, rows, lanes, parts):
        for i in range(target.shape[0]):
            target[i, rows, lanes] = parts[i]

    def start(panel):
        chunk, odd = divmod(panel, 2)
        turned[...] = ref["rows", chunk][:, span(odd)].T
        for c in range(chunk + 1):
            wide = 2 * PANEL if c < chunk else PANEL * (odd + 1)
            gram = multiply(turned[...], ref["rows", c][:, :wide]) * scale
            if c == chunk:
                gram = gram + jnp.where(diagonal(gram.shape, odd * PANEL), damp, 0.0)
            work(panel)[:, 2 * c * PANEL : 2 * c * PANEL + wide] = gram

    def solve(panel, sources):
        rows = work(panel)
        for p in sources:
            inverse = right_of(load("solve", p))
            solved = multiply(left_of(pieces(rows[:, span(p)])), inverse)
            parts = pieces(solved)
            store(lower(panel), slice(None), span(p), parts)
            store(ref["upper", panel], span(p), slice(None), pieces(solved.T))
            left = left_of(parts)
            for c in range(p + 1, panel + 1):
                right = right_of(load("upper", c, span(p)))
                rows[:, span(c)] = rows[:, span(c)] - multiply(left, right)

    def solve_half(panel, half, inverse):
        rows, p = work(panel), panel - 1
        lanes = slice(p * PANEL + half * BLOCK, p * PANEL + (half + 1) * BLOCK)
        solved = product(rows[:, lanes], inverse.T)
        flipped = solved.T
        store(lower(panel), slice(None), lanes, pieces(solved))
        store(ref["upper", panel], lanes, slice(None), pieces(flipped))
        if half == 0:
            lanes = slice(p * PANEL + BLOCK, panel * PANEL)
            rows[:, lanes] = rows[:, lanes] - product(solved, across[...])
        rows[:, span(panel)] = rows[:, span(panel)] - product(solved, flipped)

    def block(panel, row, lane):
        lanes = slice(panel * PANEL + lane * BLOCK, panel * PANEL + (lane + 1) * BLOCK)
        return work(panel)[row * BLOCK : (row + 1) * BLOCK, lanes]

    def factor(panel, half):
        value = block(panel, half, half)
        return inverse_factor([value[8 * g : 8 * g + 8, :] for g in range(BLOCK // 8)])

    def inverse_of():
        zero = jnp.zeros((BLOCK, BLOCK), f32)
        corner = -product(bottom[...], between[...])
        return jnp.concatenate(
            [
                jnp.concatenate([top[...], zero], axis=1),
                jnp.concatenate([corner, bottom[...]], axis=1),
            ],
            axis=0,
        )

    def short_sum(panel, sources):
        lanes = slice(sources[0] * PANEL, (sources[-1] + 1) * PANEL)
        high, middle = lower(panel)[0, :, lanes], lower(panel)[1, :, lanes]
        solved_high = [ref["high", p][...] for p in sources]
        solved_middle = [ref["middle", p][...] for p in sources]
        return multiply(
            jnp.concatenate([high, high, middle], axis=1),
            jnp.concatenate([*solved_high, *solved_middle, *solved_high], axis=0),
        )

    def unit(panel):
        return diagonal((PANEL, SHARE * PANEL), (panel - here * SHARE) * PANEL).astype(f32)

    def finish(panel, inverse, wanted):
        left, right = pieces(inverse), pieces(wanted)
        solved = multiply(
            jnp.concatenate([left[0], left[0], left[1]], axis=1),
            jnp.concatenate([right[0], right[1], right[0]], axis=0),
        )
        high, middle, _ = pieces(solved)
        if panel + 1 == total:
            ref["inverse"][span(panel), :] = high
        else:
            ref["high", panel][...] = high
            ref["middle", panel][...] = middle

    def finish_before(panel):
        before = panel - 1
        inverse = inverse_of()
        store(ref["solve", before], slice(None), slice(None), pieces(inverse.T))
        finish(before, inverse, ref["wanted"][...])

    def hessian(chunks):
        for chunk in chunks:
            gram = multiply(ref["here"][...], ref["rows", chunk][...]) * scale
            spread = diagonal(gram.shape, (here - chunk) * SHARE * PANEL)
            lanes = span(2 * chunk, 2)
            ref["hessian"][:, lanes] = gram + jnp.where(spread, damp, 0.0)

    def phase(body):
        pl.when(here >= 0)(body)

    first, last = panels[0], panels[-1]
    ending = last + 1 == total
    if first == 0:
        start(0)
    else:
        work(first)[:, span(first)] = ref["diagonal_in"][...]
        lower(first)[:, :, : first * PANEL] = ref["lower_in"][...]
        top[...], bottom[...], between[...] = (ref["pending_in"][i] for i in range(3))
        ref["wanted"][...] = ref["wanted_in"][...]
    if ending:
        for chunk in range(total // SHARE):

            @pl.when(here == chunk)
            def _():
                ref["here"][...] = ref["rows", chunk][...].T

    for t in panels:
        after = t + 1

        @phase
        def _():
            if t > first:
                solve_half(t, 1, bottom[...])
            made = factor(t, 0)
            if t:
                finish_before(t)
            if after < total:
                start(after)
                solve(after, range(0, t // 3))
            else:
                hessian(range(total // SHARE // 2))
            top[...] = made

        @phase
        def _():
            made_across = product(top[...], block(t, 0, 1))
            across[...] = made_across
            flipped = made_across.T
            spot = (SECOND, slice(t * PANEL + BLOCK, (t + 1) * PANEL))
            work(t)[spot] = work(t)[spot] - product(flipped, made_across)
            made = factor(t, 1)
            between[...] = product(flipped, top[...])
            if after < total:
                solve(after, range(t // 3, t))
                solve_half(after, 0, top[...])
            else:
                hessian(range(total // SHARE // 2, total // SHARE))
            ref["wanted"][...] = unit(t) - short_sum(t, range(t)) if t else unit(t)
            bottom[...] = made

    if ending:

        @phase
        def _():
            finish(last, inverse_of(), ref["wanted"][...])

        for p in range(last):
            ref["inverse"][span(p), :] = ref["high", p][...]
    else:
        after = last + 1
        solve_half(after, 1, bottom[...])
        ref["diagonal_out"][...] = work(after)[:, span(after)]
        ref["lower_out"][...] = lower(after)[:, :, : after * PANEL]
        for i, value in enumerate((top, bottom, between)):
            ref["pending_out"][i] = value[...]
        ref["wanted_out"][...] = ref["wanted"][...]


def run_panels(panels, total, here, stats, known):
    shape = jax.ShapeDtypeStruct
    first, last = panels[0], panels[-1]
    ending = last + 1 == total
    after = min(last + 1, total - 1)
    count_rows = known["rows", 0].shape[0]
    square = shape((BLOCK, BLOCK), f32)
    columns = SHARE * PANEL
    made = {}
    for t in range(max(first, 1), after + 1) if first == 0 else range(first + 1, after + 1):
        made["upper", t] = shape((3, t * PANEL, PANEL), bf16)
    for t in range(max(first - 1, 0), last):
        made["solve", t] = shape((3, PANEL, PANEL), bf16)
        made["high", t] = shape((PANEL, columns), bf16)
        made["middle", t] = shape((PANEL, columns), bf16)
    scratch = {name: square for name in ("top", "bottom", "across", "between")}
    for i in range(2):
        scratch["work", i] = shape((PANEL, (after + 1) * PANEL), f32)
        scratch["lower", i] = shape((2, PANEL, max(after, 1) * PANEL), bf16)
    scratch["wanted"] = shape((PANEL, columns), f32)
    scratch["turned"] = shape((PANEL, count_rows), bf16)
    if ending:
        outputs = {
            "hessian": shape((columns, total * PANEL), f32),
            "inverse": shape((total * PANEL, columns), bf16),
        }
        scratch.update(made)
        scratch["here"] = shape((columns, count_rows), bf16)
    else:
        outputs = {
            **made,
            "diagonal_out": shape((PANEL, PANEL), f32),
            "lower_out": shape((2, PANEL, after * PANEL), bf16),
            "pending_out": shape((3, BLOCK, BLOCK), f32),
            "wanted_out": shape((PANEL, columns), f32),
        }
    chunks = after // 2 + 1
    inputs = {n: a for n, a in known.items() if n[0] != "rows" or n[1] < chunks}
    in_vmem = pl.BlockSpec(memory_space=pltpu.VMEM)
    results = pl.pallas_call(
        functools.partial(panels_kernel, panels, total, list(inputs), list(outputs), list(scratch)),
        out_shape=list(outputs.values()),
        in_specs=[pl.BlockSpec(memory_space=pltpu.SMEM)] * 2 + [in_vmem] * len(inputs),
        out_specs=[in_vmem] * len(outputs),
        scratch_shapes=[pltpu.VMEM(a.shape, a.dtype) for a in scratch.values()],
        compiler_params=pltpu.CompilerParams(vmem_limit_bytes=56 * 2**20),
        cost_estimate=pl.CostEstimate(
            flops=15 * 10**9 * len(panels), bytes_accessed=2**23, transcendentals=0
        ),
        name=f"panels{first}to{last}",
    )(here, stats, *inputs.values())
    return dict(zip(outputs, results))


def factor(here, stats, parts, gathered, plan=((0,), (1, 2), (3, 4), (5, 6, 7))):
    known = {("rows", 0): parts[0]}
    total = plan[-1][-1] + 1
    arriving = gathered(parts[1])
    for number, panels in enumerate(plan):
        made = run_panels(panels, total, here, stats, known)
        if number + 1 < len(parts):
            known["rows", number + 1] = arriving
        if number + 2 < len(parts):
            pending = made["pending_out"]
            arriving, pending, part = lax.optimization_barrier(
                (arriving, pending, parts[number + 2])
            )
            known["rows", number + 1], made["pending_out"] = arriving, pending
            arriving = gathered(part)
        for name in ("diagonal", "lower", "pending", "wanted"):
            known.pop(name + "_in", None)
            if name + "_out" in made:
                known[name + "_in"] = made.pop(name + "_out")
        known.update(made)
    return known["hessian"], known["inverse"]


def local(tokens, routes, chosen):
    slots = chosen.shape[0]
    width = tokens.shape[1]
    flat = routes.reshape(-1)
    hits = (flat[:, None] == chosen[None, :]).astype(jnp.int32)
    before = jnp.cumsum(hits, axis=0) - hits
    slot_base = jnp.arange(slots, dtype=jnp.int32)[None, :] * MOST
    target = jnp.sum(hits * (slot_base + before), axis=1)
    named = jnp.sum(hits, axis=1)
    places = jnp.arange(slots * MOST, dtype=jnp.int32)
    picks = ((places[:, None] == target[None, :]) & (named[None, :] > 0)).astype(jnp.bfloat16)
    picks = jnp.sum(picks.reshape(slots * MOST, routes.shape[0], routes.shape[1]), axis=2)
    chunk = SHARE * PANEL

    def routed(columns):
        outgoing = jnp.dot(picks, columns, preferred_element_type=f32).astype(bf16)
        outgoing = outgoing.reshape(slots, MOST, -1)
        arrived = lax.all_to_all(outgoing, "expert", split_axis=0, concat_axis=0, tiled=True)
        return arrived.reshape(slots * MOST, -1)

    def gathered(rows):
        return lax.all_gather(rows, "helper", axis=0, tiled=True)

    head = routed(tokens[:, :chunk])
    first = gathered(head)
    head, rest = lax.optimization_barrier((head, tokens[:, chunk:]))
    tail = routed(rest)
    live = jnp.any(head != 0, axis=1) | jnp.any(tail != 0, axis=1)
    trace = sum(jnp.sum(jnp.square(part.astype(f32))) for part in (head, tail))
    live, trace = lax.psum((jnp.sum(live.astype(f32)), trace), "helper")
    scale = 2.0 / live
    stats = jnp.stack([scale, 0.01 * scale * trace / width])
    here = lax.axis_index("helper").astype(jnp.int32).reshape(1)
    first, tail = lax.optimization_barrier((first, tail))
    parts = [first] + [tail[:, i : i + chunk] for i in range(0, width - chunk, chunk)]
    hessian, inverse = factor(here, stats, parts, gathered)
    return (hessian[None], inverse[None])


def solution(mesh):
    placed = (P(("expert", "helper"), None), P(("expert", "helper"), None), P())
    return jax.shard_map(
        local,
        mesh=mesh,
        in_specs=placed,
        out_specs=(P("expert", "helper", None), P("expert", None, "helper")),
        check_vma=False,
    )
```

```python
import functools

import jax
import jax.numpy as jnp
from jax import lax
from jax.experimental import pallas as pl
from jax.experimental.pallas import tpu as pltpu
from jax.sharding import PartitionSpec as P

MOST = 4
BLOCK = 128
PANEL = 256
SHARE = 2
CHUNK = 4
CHAIN = 8

f32 = jnp.float32
bf16 = jnp.bfloat16


def multiply(left, right):
    return jnp.dot(left, right, preferred_element_type=f32)


def pieces(value):
    high = value.astype(bf16)
    rest = value - high.astype(f32)
    middle = rest.astype(bf16)
    return high, middle, (rest - middle.astype(f32)).astype(bf16)


def left_of(parts):
    high, middle, low = parts
    return jnp.concatenate([high, high, middle, middle, high, low], axis=1)


def right_of(parts):
    high, middle, low = parts
    return jnp.concatenate([high, middle, high, middle, low, high], axis=0)


def product(left, right):
    return multiply(left_of(pieces(left)), right_of(pieces(right)))


def spread_row(group, row):
    return jnp.broadcast_to(group[row : row + 1, :], group.shape)


def spread_lane(group, lane):
    return jnp.broadcast_to(group[:, lane : lane + 1], group.shape)


def inverse_factor(groups):
    groups = list(groups)
    row = lax.broadcasted_iota(jnp.int32, (8, BLOCK), 0)
    lane = lax.broadcasted_iota(jnp.int32, (8, BLOCK), 1)
    below = [row > j for j in range(8)]
    result = []
    for first in range(len(groups)):
        base = 8 * first
        columns = [spread_lane(groups[first], base + k) for k in range(8)]
        scales, norms, heads, factors = [], [], [], []
        for j in range(8):
            pivot = spread_row(columns[j], j)
            scales.append(1.0 / pivot)
            norms.append(lax.rsqrt(pivot))
            heads.append([spread_row(columns[k], j) for k in range(j + 1, 8)])
            under = jnp.where(below[j], columns[j], 0.0)
            factors.append(under * scales[j])
            for k in range(j + 1, 8):
                columns[k] = columns[k] - (under * heads[j][k - j - 1]) * scales[j]
        pivot_rows = []
        own = groups[first]
        for j in range(8):
            hit = lane == base + j
            pivot_row = jnp.where(hit, 1.0, spread_row(own, j))
            pivot_rows.append(jnp.where((lane > base + j) & (lane < base + 8), 0.0, pivot_row))
            if j < 7:
                own = jnp.where(hit & below[j], 0.0, own) - factors[j] * pivot_row
        inside = (lane >= base) & (lane < base + 8)
        for g in range(first + 1, len(groups)):
            columns = [spread_lane(groups[g], base + k) for k in range(8)]
            rest = jnp.where(inside, 0.0, groups[g])
            for j in range(8):
                factor = columns[j] * scales[j]
                for k in range(j + 1, 8):
                    columns[k] = columns[k] - factor * heads[j][k - j - 1]
                rest = rest - factor * pivot_rows[j]
            groups[g] = rest
        norm = norms[0]
        for j in range(1, 8):
            norm = jnp.where(row == j, norms[j], norm)
        unit = jnp.where(lane < row + base, own, 0.0)
        result.append(jnp.where(lane == row + base, 1.0, unit) * norm)
    return jnp.concatenate(result, axis=0)


def diagonal(shape, offset):
    row = lax.broadcasted_iota(jnp.int32, shape, 0) + offset
    return row == lax.broadcasted_iota(jnp.int32, shape, 1)


def span(panel, number=1):
    return slice(panel * PANEL, (panel + number) * PANEL)


FIRST, SECOND = slice(0, BLOCK), slice(BLOCK, PANEL)


def panels_kernel(panels, total, inputs, outputs, scratch, here_ref, *refs):
    names = [*inputs, *outputs, *scratch]
    ref = dict(zip(names, refs))
    here = here_ref[0]
    if panels[0] == 0:
        sums = ref["rows", 0][:, CHUNK * PANEL :].astype(f32)
        sums = jnp.sum(sums, axis=0, keepdims=True)
        scale = 2.0 / sums[:, 3:4]
        trace = sums[:, 0:1] + (sums[:, 1:2] + sums[:, 2:3])
        damp = 0.01 * scale * trace / (total * PANEL)
        ref["stats"][...] = jnp.concatenate(
            [jnp.broadcast_to(value, (8, BLOCK)) for value in (scale, damp)], axis=0
        )
    scale, damp = ref["stats"][0:1, 0:1], ref["stats"][8:9, 0:1]
    top, bottom, across, between = (ref[n] for n in ("top", "bottom", "across", "between"))
    turned = ref["turned"]

    def work(panel):
        return ref["work", panel % 2]

    def lower(panel):
        return ref["lower", panel % 2]

    def load(name, panel, rows=slice(None), lanes=slice(None)):
        return [ref[name, panel][i, rows, lanes] for i in range(3)]

    def store(target, rows, lanes, parts):
        for i in range(target.shape[0]):
            target[i, rows, lanes] = parts[i]

    def start(panel):
        chunk, place = divmod(panel, CHUNK)
        turned[...] = ref["rows", chunk][:, span(place)].T
        for c in range(chunk + 1):
            number = CHUNK if c < chunk else place + 1
            gram = multiply(turned[...], ref["rows", c][:, span(0, number)]) * scale
            if c == chunk:
                gram = gram + jnp.where(diagonal(gram.shape, place * PANEL), damp, 0.0)
            work(panel)[:, span(CHUNK * c, number)] = gram

    def solve(panel, sources):
        rows = work(panel)
        for p in sources:
            inverse = right_of(load("solve", p))
            solved = multiply(left_of(pieces(rows[:, span(p)])), inverse)
            parts = pieces(solved)
            store(lower(panel), slice(None), span(p), parts)
            store(ref["upper", panel], span(p), slice(None), pieces(solved.T))
            left = left_of(parts)
            for c in range(p + 1, panel + 1):
                right = right_of(load("upper", c, span(p)))
                rows[:, span(c)] = rows[:, span(c)] - multiply(left, right)

    def solve_half(panel, half, inverse):
        rows, p = work(panel), panel - 1
        lanes = slice(p * PANEL + half * BLOCK, p * PANEL + (half + 1) * BLOCK)
        solved = product(rows[:, lanes], inverse.T)
        flipped = solved.T
        store(lower(panel), slice(None), lanes, pieces(solved))
        store(ref["upper", panel], lanes, slice(None), pieces(flipped))
        if half == 0:
            lanes = slice(p * PANEL + BLOCK, panel * PANEL)
            rows[:, lanes] = rows[:, lanes] - product(solved, across[...])
        rows[:, span(panel)] = rows[:, span(panel)] - product(solved, flipped)

    def block(panel, row, lane):
        lanes = slice(panel * PANEL + lane * BLOCK, panel * PANEL + (lane + 1) * BLOCK)
        return work(panel)[row * BLOCK : (row + 1) * BLOCK, lanes]

    def factor(panel, half):
        value = block(panel, half, half)
        return inverse_factor([value[8 * g : 8 * g + 8, :] for g in range(BLOCK // 8)])

    def inverse_of():
        zero = jnp.zeros((BLOCK, BLOCK), f32)
        corner = -product(bottom[...], between[...])
        return jnp.concatenate(
            [
                jnp.concatenate([top[...], zero], axis=1),
                jnp.concatenate([corner, bottom[...]], axis=1),
            ],
            axis=0,
        )

    def short_sum(panel, sources):
        lanes = slice(sources[0] * PANEL, (sources[-1] + 1) * PANEL)
        high, middle = lower(panel)[0, :, lanes], lower(panel)[1, :, lanes]
        solved_high = [ref["high", p][...] for p in sources]
        solved_middle = [ref["middle", p][...] for p in sources]
        return multiply(
            jnp.concatenate([high, high, middle], axis=1),
            jnp.concatenate([*solved_high, *solved_middle, *solved_high], axis=0),
        )

    def unit(panel):
        return diagonal((PANEL, SHARE * PANEL), (panel - here * SHARE) * PANEL).astype(f32)

    def finish(panel, inverse, wanted):
        left, right = pieces(inverse), pieces(wanted)
        solved = multiply(
            jnp.concatenate([left[0], left[0], left[1]], axis=1),
            jnp.concatenate([right[0], right[1], right[0]], axis=0),
        )
        high, middle, _ = pieces(solved)
        if panel + 1 == total:
            ref["inverse"][span(panel), :] = high
        else:
            ref["high", panel][...] = high
            ref["middle", panel][...] = middle

    def finish_before(panel):
        before = panel - 1
        inverse = inverse_of()
        store(ref["solve", before], slice(None), slice(None), pieces(inverse.T))
        finish(before, inverse, ref["wanted"][...])

    def hessian(chunk):
        gram = multiply(ref["here"][...], ref["rows", chunk][:, span(0, CHUNK)]) * scale
        spread = diagonal(gram.shape, (here * SHARE - chunk * CHUNK) * PANEL)
        ref["hessian"][:, span(CHUNK * chunk, CHUNK)] = gram + jnp.where(spread, damp, 0.0)

    def phase(body):
        pl.when(here >= 0)(body)

    first, last = panels[0], panels[-1]
    ending = last + 1 == total
    if first == 0:
        start(0)
    else:
        work(first)[:, span(first)] = ref["diagonal_in"][...]
        lower(first)[:, :, : first * PANEL] = ref["lower_in"][...]
        top[...], bottom[...], between[...] = (ref["pending_in"][i] for i in range(3))
        ref["wanted"][...] = ref["wanted_in"][...]
    if ending:
        for helper in range(total // SHARE):

            @pl.when(here == helper)
            def _():
                chunk, place = divmod(helper * SHARE, CHUNK)
                ref["here"][...] = ref["rows", chunk][:, span(place, SHARE)].T

    for t in panels:
        after = t + 1

        @phase
        def _():
            if t > first:
                solve_half(t, 1, bottom[...])
            made = factor(t, 0)
            if t:
                finish_before(t)
            if after < total:
                start(after)
                solve(after, range(0, t // 3))
            else:
                hessian(0)
            top[...] = made

        @phase
        def _():
            made_across = product(top[...], block(t, 0, 1))
            across[...] = made_across
            flipped = made_across.T
            spot = (SECOND, slice(t * PANEL + BLOCK, (t + 1) * PANEL))
            work(t)[spot] = work(t)[spot] - product(flipped, made_across)
            made = factor(t, 1)
            between[...] = product(flipped, top[...])
            if after < total:
                solve(after, range(t // 3, t))
                solve_half(after, 0, top[...])
            else:
                hessian(1)
            ref["wanted"][...] = unit(t) - short_sum(t, range(t)) if t else unit(t)
            bottom[...] = made

    if ending:

        @phase
        def _():
            finish(last, inverse_of(), ref["wanted"][...])

        for p in range(last):
            ref["inverse"][span(p), :] = ref["high", p][...]
    else:
        after = last + 1
        solve_half(after, 1, bottom[...])
        ref["diagonal_out"][...] = work(after)[:, span(after)]
        ref["lower_out"][...] = lower(after)[:, :, : after * PANEL]
        for i, value in enumerate((top, bottom, between)):
            ref["pending_out"][i] = value[...]
        ref["wanted_out"][...] = ref["wanted"][...]


def run_panels(panels, total, here, known):
    shape = jax.ShapeDtypeStruct
    first, last = panels[0], panels[-1]
    ending = last + 1 == total
    after = min(last + 1, total - 1)
    count_rows = known["rows", 0].shape[0]
    square = shape((BLOCK, BLOCK), f32)
    columns = SHARE * PANEL
    made = {}
    for t in range(max(first, 1), after + 1) if first == 0 else range(first + 1, after + 1):
        made["upper", t] = shape((3, t * PANEL, PANEL), bf16)
    for t in range(max(first - 1, 0), last):
        made["solve", t] = shape((3, PANEL, PANEL), bf16)
        made["high", t] = shape((PANEL, columns), bf16)
        made["middle", t] = shape((PANEL, columns), bf16)
    scratch = {name: square for name in ("top", "bottom", "across", "between")}
    for i in range(2):
        scratch["work", i] = shape((PANEL, (after + 1) * PANEL), f32)
        scratch["lower", i] = shape((2, PANEL, max(after, 1) * PANEL), bf16)
    scratch["wanted"] = shape((PANEL, columns), f32)
    scratch["turned"] = shape((PANEL, count_rows), bf16)
    if ending:
        outputs = {
            "hessian": shape((columns, total * PANEL), f32),
            "inverse": shape((total * PANEL, columns), bf16),
        }
        scratch.update(made)
        scratch["here"] = shape((columns, count_rows), bf16)
    else:
        outputs = {
            **made,
            "diagonal_out": shape((PANEL, PANEL), f32),
            "lower_out": shape((2, PANEL, after * PANEL), bf16),
            "pending_out": shape((3, BLOCK, BLOCK), f32),
            "wanted_out": shape((PANEL, columns), f32),
        }
    if first == 0:
        outputs["stats"] = shape((16, BLOCK), f32)
    chunks = after // CHUNK + 1
    inputs = {n: a for n, a in known.items() if n[0] != "rows" or n[1] < chunks}
    in_vmem = pl.BlockSpec(memory_space=pltpu.VMEM)
    results = pl.pallas_call(
        functools.partial(panels_kernel, panels, total, list(inputs), list(outputs), list(scratch)),
        out_shape=list(outputs.values()),
        in_specs=[pl.BlockSpec(memory_space=pltpu.SMEM)] + [in_vmem] * len(inputs),
        out_specs=[in_vmem] * len(outputs),
        scratch_shapes=[pltpu.VMEM(a.shape, a.dtype) for a in scratch.values()],
        compiler_params=pltpu.CompilerParams(vmem_limit_bytes=56 * 2**20),
        cost_estimate=pl.CostEstimate(
            flops=14 * 10**9 * len(panels), bytes_accessed=2**23, transcendentals=0
        ),
        name=f"panels{first}to{last}",
    )(here, *inputs.values())
    return dict(zip(outputs, results))


def factor(here, first, second):
    total = 2 * CHUNK
    known = {("rows", 0): first}
    made = run_panels((0, 1, 2), total, here, known)
    for name in ("diagonal", "lower", "pending", "wanted"):
        known[name + "_in"] = made.pop(name + "_out")
    known.update(made)
    known["rows", 1] = second
    made = run_panels((3, 4, 5, 6, 7), total, here, known)
    return made["hessian"], made["inverse"]


def of_group(value, axis):
    number = lax.axis_size("helper")
    blocks = [value]
    for step in range(1, number):
        pairs = [(i, (i + step) % number) for i in range(number)]
        blocks.append(lax.ppermute(value, "helper", pairs))
    return jnp.concatenate(blocks, axis=axis)


def local(tokens, routes, chosen):
    slots = chosen.shape[0]
    block = tokens.shape[0]
    half = tokens.shape[1] // 2
    group_routes = of_group(routes.T, 1)
    group_tokens = of_group(tokens, 0)
    number = group_tokens.shape[0]
    named = jnp.any(group_routes[None, :, :] == chosen[:, None, None], axis=1)
    place = jnp.arange(number, dtype=jnp.int32)
    earlier = (place[:, None] < place[None, :]) & (place[:, None] // block == place[None, :] // block)
    before = jnp.dot(named.astype(bf16), earlier.astype(bf16), preferred_element_type=f32)
    spot = before.astype(jnp.int32) + place // block * MOST
    spots = jnp.arange(number // block * MOST, dtype=jnp.int32)
    picks = named[:, None, :] & (spot[:, None, :] == spots[None, :, None])
    picks = picks.astype(bf16).reshape(slots * spots.shape[0], number)

    def routed(columns):
        outgoing = multiply(picks, columns).astype(bf16)
        outgoing = outgoing.reshape(slots, spots.shape[0], -1)
        arrived = lax.all_to_all(outgoing, "expert", split_axis=0, concat_axis=0, tiled=True)
        return arrived.reshape(slots * spots.shape[0], -1)

    rest = jnp.sum(jnp.square(group_tokens.astype(f32)), axis=1, keepdims=True)
    notes = []
    for _ in range(3):
        piece = lax.reduce_precision(rest, 8, 7)
        notes.append(piece)
        rest = rest - piece
    notes.append(jnp.ones_like(rest))
    notes = jnp.pad(jnp.concatenate(notes, axis=1), ((0, 0), (0, BLOCK - len(notes)))).astype(bf16)
    first = routed(jnp.concatenate([group_tokens[:, :half], notes], axis=1))
    first, columns = lax.optimization_barrier((first, group_tokens[:, half:]))
    second = routed(columns)
    here = lax.axis_index("helper").astype(jnp.int32).reshape(1)
    hessian, inverse = factor(here, first, second)
    return (hessian[None], inverse[None])


def solution(mesh):
    placed = (P(("expert", "helper"), None), P(("expert", "helper"), None), P())
    return jax.shard_map(
        local,
        mesh=mesh,
        in_specs=placed,
        out_specs=(P("expert", "helper", None), P("expert", None, "helper")),
        check_vma=False,
    )
```

```python
import functools

import jax
import jax.numpy as jnp
from jax import lax
from jax.experimental import pallas as pl
from jax.experimental.pallas import tpu as pltpu
from jax.sharding import PartitionSpec as P

MOST = 4
NOTES = 8
BLOCK = 128
PANEL = 256
SHARE = 2
CHUNK = 4
CHAIN = 8

f32 = jnp.float32
bf16 = jnp.bfloat16


def multiply(left, right):
    return jnp.dot(left, right, preferred_element_type=f32)


def pieces(value):
    high = value.astype(bf16)
    rest = value - high.astype(f32)
    middle = rest.astype(bf16)
    return high, middle, (rest - middle.astype(f32)).astype(bf16)


def left_of(parts):
    high, middle, low = parts
    return jnp.concatenate([high, high, middle, middle, high, low], axis=1)


def right_of(parts):
    high, middle, low = parts
    return jnp.concatenate([high, middle, high, middle, low, high], axis=0)


def product(left, right):
    return multiply(left_of(pieces(left)), right_of(pieces(right)))


def spread_row(group, row):
    return jnp.broadcast_to(group[row : row + 1, :], group.shape)


def spread_lane(group, lane):
    return jnp.broadcast_to(group[:, lane : lane + 1], group.shape)


def inverse_factor(groups):
    groups = list(groups)
    row = lax.broadcasted_iota(jnp.int32, (8, BLOCK), 0)
    lane = lax.broadcasted_iota(jnp.int32, (8, BLOCK), 1)
    below = [row > j for j in range(8)]
    result = []
    for first in range(len(groups)):
        base = 8 * first
        columns = [spread_lane(groups[first], base + k) for k in range(8)]
        scales, norms, heads, factors = [], [], [], []
        for j in range(8):
            pivot = spread_row(columns[j], j)
            scales.append(1.0 / pivot)
            norms.append(lax.rsqrt(pivot))
            heads.append([spread_row(columns[k], j) for k in range(j + 1, 8)])
            under = jnp.where(below[j], columns[j], 0.0)
            factors.append(under * scales[j])
            for k in range(j + 1, 8):
                columns[k] = columns[k] - (under * heads[j][k - j - 1]) * scales[j]
        pivot_rows = []
        own = groups[first]
        for j in range(8):
            hit = lane == base + j
            pivot_row = jnp.where(hit, 1.0, spread_row(own, j))
            pivot_rows.append(jnp.where((lane > base + j) & (lane < base + 8), 0.0, pivot_row))
            if j < 7:
                own = jnp.where(hit & below[j], 0.0, own) - factors[j] * pivot_row
        inside = (lane >= base) & (lane < base + 8)
        for g in range(first + 1, len(groups)):
            columns = [spread_lane(groups[g], base + k) for k in range(8)]
            rest = jnp.where(inside, 0.0, groups[g])
            for j in range(8):
                factor = columns[j] * scales[j]
                for k in range(j + 1, 8):
                    columns[k] = columns[k] - factor * heads[j][k - j - 1]
                rest = rest - factor * pivot_rows[j]
            groups[g] = rest
        norm = norms[0]
        for j in range(1, 8):
            norm = jnp.where(row == j, norms[j], norm)
        unit = jnp.where(lane < row + base, own, 0.0)
        result.append(jnp.where(lane == row + base, 1.0, unit) * norm)
    return jnp.concatenate(result, axis=0)


def diagonal(shape, offset):
    row = lax.broadcasted_iota(jnp.int32, shape, 0) + offset
    return row == lax.broadcasted_iota(jnp.int32, shape, 1)


def span(panel, number=1):
    return slice(panel * PANEL, (panel + number) * PANEL)


FIRST, SECOND = slice(0, BLOCK), slice(BLOCK, PANEL)


def panels_kernel(panels, total, inputs, outputs, scratch, here_ref, *refs):
    names = [*inputs, *outputs, *scratch]
    ref = dict(zip(names, refs))
    here = here_ref[0]
    if panels[0] == 0:
        sums = ref["rows", 0][:, CHUNK * PANEL :].astype(f32)
        sums = jnp.sum(sums, axis=0, keepdims=True)
        count, *norms = (sums[:, i : i + 1] for i in range(NOTES, NOTES + 4))
        scale = 2.0 / count
        trace = norms[0] + (norms[1] + norms[2])
        damp = 0.01 * scale * trace / (total * PANEL)
        ref["stats"][...] = jnp.concatenate(
            [jnp.broadcast_to(value, (8, BLOCK)) for value in (scale, damp)], axis=0
        )
    scale, damp = ref["stats"][0:1, 0:1], ref["stats"][8:9, 0:1]
    top, bottom, across, between = (ref[n] for n in ("top", "bottom", "across", "between"))
    turned = ref["turned"]

    def work(panel):
        return ref["work", panel % 2]

    def lower(panel):
        return ref["lower", panel % 2]

    def load(name, panel, rows=slice(None), lanes=slice(None)):
        return [ref[name, panel][i, rows, lanes] for i in range(3)]

    def store(target, rows, lanes, parts):
        for i in range(target.shape[0]):
            target[i, rows, lanes] = parts[i]

    def start(panel):
        chunk, place = divmod(panel, CHUNK)
        turned[...] = ref["rows", chunk][:, span(place)].T
        for c in range(chunk + 1):
            number = CHUNK if c < chunk else place + 1
            gram = multiply(turned[...], ref["rows", c][:, span(0, number)]) * scale
            if c == chunk:
                gram = gram + jnp.where(diagonal(gram.shape, place * PANEL), damp, 0.0)
            work(panel)[:, span(CHUNK * c, number)] = gram

    def solve(panel, sources):
        rows = work(panel)
        for p in sources:
            inverse = right_of(load("solve", p))
            solved = multiply(left_of(pieces(rows[:, span(p)])), inverse)
            parts = pieces(solved)
            store(lower(panel), slice(None), span(p), parts)
            store(ref["upper", panel], span(p), slice(None), pieces(solved.T))
            left = left_of(parts)
            for c in range(p + 1, panel + 1):
                right = right_of(load("upper", c, span(p)))
                rows[:, span(c)] = rows[:, span(c)] - multiply(left, right)

    def solve_half(panel, half, inverse):
        rows, p = work(panel), panel - 1
        lanes = slice(p * PANEL + half * BLOCK, p * PANEL + (half + 1) * BLOCK)
        solved = product(rows[:, lanes], inverse.T)
        flipped = solved.T
        store(lower(panel), slice(None), lanes, pieces(solved))
        store(ref["upper", panel], lanes, slice(None), pieces(flipped))
        if half == 0:
            lanes = slice(p * PANEL + BLOCK, panel * PANEL)
            rows[:, lanes] = rows[:, lanes] - product(solved, across[...])
        rows[:, span(panel)] = rows[:, span(panel)] - product(solved, flipped)

    def block(panel, row, lane):
        lanes = slice(panel * PANEL + lane * BLOCK, panel * PANEL + (lane + 1) * BLOCK)
        return work(panel)[row * BLOCK : (row + 1) * BLOCK, lanes]

    def factor(panel, half):
        value = block(panel, half, half)
        return inverse_factor([value[8 * g : 8 * g + 8, :] for g in range(BLOCK // 8)])

    def inverse_of():
        zero = jnp.zeros((BLOCK, BLOCK), f32)
        corner = -product(bottom[...], between[...])
        return jnp.concatenate(
            [
                jnp.concatenate([top[...], zero], axis=1),
                jnp.concatenate([corner, bottom[...]], axis=1),
            ],
            axis=0,
        )

    def short_sum(panel, sources):
        lanes = slice(sources[0] * PANEL, (sources[-1] + 1) * PANEL)
        high, middle = lower(panel)[0, :, lanes], lower(panel)[1, :, lanes]
        solved_high = [ref["high", p][...] for p in sources]
        solved_middle = [ref["middle", p][...] for p in sources]
        return multiply(
            jnp.concatenate([high, high, middle], axis=1),
            jnp.concatenate([*solved_high, *solved_middle, *solved_high], axis=0),
        )

    def unit(panel):
        return diagonal((PANEL, SHARE * PANEL), (panel - here * SHARE) * PANEL).astype(f32)

    def finish(panel, inverse, wanted):
        left, right = pieces(inverse), pieces(wanted)
        solved = multiply(
            jnp.concatenate([left[0], left[0], left[1]], axis=1),
            jnp.concatenate([right[0], right[1], right[0]], axis=0),
        )
        high, middle, _ = pieces(solved)
        if panel + 1 == total:
            ref["inverse"][span(panel), :] = high
        else:
            ref["high", panel][...] = high
            ref["middle", panel][...] = middle

    def finish_before(panel):
        before = panel - 1
        inverse = inverse_of()
        store(ref["solve", before], slice(None), slice(None), pieces(inverse.T))
        finish(before, inverse, ref["wanted"][...])

    def hessian(chunk):
        gram = multiply(ref["here"][...], ref["rows", chunk][:, span(0, CHUNK)]) * scale
        spread = diagonal(gram.shape, (here * SHARE - chunk * CHUNK) * PANEL)
        ref["hessian"][:, span(CHUNK * chunk, CHUNK)] = gram + jnp.where(spread, damp, 0.0)

    def phase(body):
        pl.when(here >= 0)(body)

    first, last = panels[0], panels[-1]
    ending = last + 1 == total
    if first == 0:
        start(0)
    else:
        work(first)[:, span(first)] = ref["diagonal_in"][...]
        lower(first)[:, :, : first * PANEL] = ref["lower_in"][...]
        top[...], bottom[...], between[...] = (ref["pending_in"][i] for i in range(3))
        ref["wanted"][...] = ref["wanted_in"][...]
    if ending:
        for helper in range(total // SHARE):

            @pl.when(here == helper)
            def _():
                chunk, place = divmod(helper * SHARE, CHUNK)
                ref["here"][...] = ref["rows", chunk][:, span(place, SHARE)].T

    for t in panels:
        after = t + 1

        @phase
        def _():
            if t > first:
                solve_half(t, 1, bottom[...])
            made = factor(t, 0)
            if t:
                finish_before(t)
            if after < total:
                start(after)
                solve(after, range(0, t // 2))
            else:
                hessian(0)
            top[...] = made

        @phase
        def _():
            made_across = product(top[...], block(t, 0, 1))
            across[...] = made_across
            flipped = made_across.T
            spot = (SECOND, slice(t * PANEL + BLOCK, (t + 1) * PANEL))
            work(t)[spot] = work(t)[spot] - product(flipped, made_across)
            made = factor(t, 1)
            between[...] = product(flipped, top[...])
            if after < total:
                solve(after, range(t // 2, t))
                solve_half(after, 0, top[...])
            else:
                hessian(1)
            ref["wanted"][...] = unit(t) - short_sum(t, range(t)) if t else unit(t)
            bottom[...] = made

    if ending:

        @phase
        def _():
            finish(last, inverse_of(), ref["wanted"][...])

        for p in range(last):
            ref["inverse"][span(p), :] = ref["high", p][...]
    else:
        after = last + 1
        solve_half(after, 1, bottom[...])
        ref["diagonal_out"][...] = work(after)[:, span(after)]
        ref["lower_out"][...] = lower(after)[:, :, : after * PANEL]
        for i, value in enumerate((top, bottom, between)):
            ref["pending_out"][i] = value[...]
        ref["wanted_out"][...] = ref["wanted"][...]


def run_panels(panels, total, here, known):
    shape = jax.ShapeDtypeStruct
    first, last = panels[0], panels[-1]
    ending = last + 1 == total
    after = min(last + 1, total - 1)
    count_rows = known["rows", 0].shape[0]
    square = shape((BLOCK, BLOCK), f32)
    columns = SHARE * PANEL
    made = {}
    for t in range(max(first, 1), after + 1) if first == 0 else range(first + 1, after + 1):
        made["upper", t] = shape((3, t * PANEL, PANEL), bf16)
    for t in range(max(first - 1, 0), last):
        made["solve", t] = shape((3, PANEL, PANEL), bf16)
        made["high", t] = shape((PANEL, columns), bf16)
        made["middle", t] = shape((PANEL, columns), bf16)
    scratch = {name: square for name in ("top", "bottom", "across", "between")}
    for i in range(2):
        scratch["work", i] = shape((PANEL, (after + 1) * PANEL), f32)
        scratch["lower", i] = shape((2, PANEL, max(after, 1) * PANEL), bf16)
    scratch["wanted"] = shape((PANEL, columns), f32)
    scratch["turned"] = shape((PANEL, count_rows), bf16)
    if ending:
        outputs = {
            "hessian": shape((columns, total * PANEL), f32),
            "inverse": shape((total * PANEL, columns), bf16),
        }
        scratch.update(made)
        scratch["here"] = shape((columns, count_rows), bf16)
    else:
        outputs = {
            **made,
            "diagonal_out": shape((PANEL, PANEL), f32),
            "lower_out": shape((2, PANEL, after * PANEL), bf16),
            "pending_out": shape((3, BLOCK, BLOCK), f32),
            "wanted_out": shape((PANEL, columns), f32),
        }
    if first == 0:
        outputs["stats"] = shape((16, BLOCK), f32)
    chunks = after // CHUNK + 1
    inputs = {n: a for n, a in known.items() if n[0] != "rows" or n[1] < chunks}
    in_vmem = pl.BlockSpec(memory_space=pltpu.VMEM)
    results = pl.pallas_call(
        functools.partial(panels_kernel, panels, total, list(inputs), list(outputs), list(scratch)),
        out_shape=list(outputs.values()),
        in_specs=[pl.BlockSpec(memory_space=pltpu.SMEM)] + [in_vmem] * len(inputs),
        out_specs=[in_vmem] * len(outputs),
        scratch_shapes=[pltpu.VMEM(a.shape, a.dtype) for a in scratch.values()],
        compiler_params=pltpu.CompilerParams(vmem_limit_bytes=56 * 2**20),
        cost_estimate=pl.CostEstimate(
            flops=14 * 10**9 * len(panels), bytes_accessed=2**23, transcendentals=0
        ),
        name=f"panels{first}to{last}",
    )(here, *inputs.values())
    return dict(zip(outputs, results))


def factor(here, first, second):
    total = 2 * CHUNK
    known = {("rows", 0): first}
    made = run_panels((0, 1, 2), total, here, known)
    for name in ("diagonal", "lower", "pending", "wanted"):
        known[name + "_in"] = made.pop(name + "_out")
    known.update(made)
    known["rows", 1] = second
    made = run_panels((3, 4, 5, 6, 7), total, here, known)
    return made["hessian"], made["inverse"]


def of_group(value):
    number = lax.axis_size("helper")
    blocks = [value]
    for step in range(1, number):
        pairs = [(i, (i + step) % number) for i in range(number)]
        blocks.append(lax.ppermute(value, "helper", pairs))
    return jnp.concatenate(blocks, axis=0)


def local(tokens, routes, chosen):
    slots = chosen.shape[0]
    block = tokens.shape[0]
    half = tokens.shape[1] // 2
    rest = jnp.sum(jnp.square(tokens.astype(f32)), axis=1, keepdims=True)
    notes = [routes.astype(f32), jnp.ones_like(rest)]
    for _ in range(3):
        piece = lax.reduce_precision(rest, 8, 7)
        notes.append(piece)
        rest = rest - piece
    notes = jnp.concatenate(notes, axis=1)
    notes = jnp.pad(notes, ((0, 0), (0, BLOCK - notes.shape[1]))).astype(bf16)
    group = of_group(jnp.concatenate([tokens[:, :half], notes, tokens[:, half:]], axis=1))
    cut = half + BLOCK
    number = group.shape[0]
    group_routes = group[:, half : half + NOTES].astype(jnp.int32).T
    named = jnp.any(group_routes[None, :, :] == chosen[:, None, None], axis=1)
    place = jnp.arange(number, dtype=jnp.int32)
    earlier = (place[:, None] < place[None, :]) & (place[:, None] // block == place[None, :] // block)
    before = jnp.dot(named.astype(bf16), earlier.astype(bf16), preferred_element_type=f32)
    spot = before.astype(jnp.int32) + place // block * MOST
    spots = jnp.arange(number // block * MOST, dtype=jnp.int32)
    picks = named[:, None, :] & (spot[:, None, :] == spots[None, :, None])
    picks = picks.astype(bf16).reshape(slots * spots.shape[0], number)

    def routed(columns):
        outgoing = multiply(picks, columns).astype(bf16)
        outgoing = outgoing.reshape(slots, spots.shape[0], -1)
        arrived = lax.all_to_all(outgoing, "expert", split_axis=0, concat_axis=0, tiled=True)
        return arrived.reshape(slots * spots.shape[0], -1)

    first = routed(group[:, :cut])
    first, columns = lax.optimization_barrier((first, group[:, cut:]))
    second = routed(columns)
    here = lax.axis_index("helper").astype(jnp.int32).reshape(1)
    hessian, inverse = factor(here, first, second)
    return (hessian[None], inverse[None])


def solution(mesh):
    placed = (P(("expert", "helper"), None), P(("expert", "helper"), None), P())
    return jax.shard_map(
        local,
        mesh=mesh,
        in_specs=placed,
        out_specs=(P("expert", "helper", None), P("expert", None, "helper")),
        check_vma=False,
    )
```

```python
import functools

import jax
import jax.numpy as jnp
from jax import lax
from jax.experimental import pallas as pl
from jax.experimental.pallas import tpu as pltpu
from jax.sharding import PartitionSpec as P

MOST = 4
NOTES = 8
BLOCK = 128
PANEL = 256
SHARE = 2
CHUNK = 4
CHAIN = 8

f32 = jnp.float32
bf16 = jnp.bfloat16


def multiply(left, right):
    return jnp.dot(left, right, preferred_element_type=f32)


def pieces(value):
    high = value.astype(bf16)
    rest = value - high.astype(f32)
    middle = rest.astype(bf16)
    return high, middle, (rest - middle.astype(f32)).astype(bf16)


def left_of(parts):
    high, middle, low = parts
    return jnp.concatenate([high, high, middle, middle, high, low], axis=1)


def right_of(parts):
    high, middle, low = parts
    return jnp.concatenate([high, middle, high, middle, low, high], axis=0)


def product(left, right):
    return multiply(left_of(pieces(left)), right_of(pieces(right)))


def spread_row(group, row):
    return jnp.broadcast_to(group[row : row + 1, :], group.shape)


def spread_lane(group, lane):
    return jnp.broadcast_to(group[:, lane : lane + 1], group.shape)


def inverse_factor(groups):
    groups = list(groups)
    row = lax.broadcasted_iota(jnp.int32, (8, BLOCK), 0)
    lane = lax.broadcasted_iota(jnp.int32, (8, BLOCK), 1)
    below = [row > j for j in range(8)]
    result = []
    for first in range(len(groups)):
        base = 8 * first
        columns = [spread_lane(groups[first], base + k) for k in range(8)]
        scales, norms, heads, factors = [], [], [], []
        for j in range(8):
            pivot = spread_row(columns[j], j)
            scales.append(1.0 / pivot)
            norms.append(lax.rsqrt(pivot))
            heads.append([spread_row(columns[k], j) for k in range(j + 1, 8)])
            under = jnp.where(below[j], columns[j], 0.0)
            factors.append(under * scales[j])
            for k in range(j + 1, 8):
                columns[k] = columns[k] - (under * heads[j][k - j - 1]) * scales[j]
        pivot_rows = []
        own = groups[first]
        for j in range(8):
            hit = lane == base + j
            pivot_row = jnp.where(hit, 1.0, spread_row(own, j))
            pivot_rows.append(jnp.where((lane > base + j) & (lane < base + 8), 0.0, pivot_row))
            if j < 7:
                own = jnp.where(hit & below[j], 0.0, own) - factors[j] * pivot_row
        inside = (lane >= base) & (lane < base + 8)
        for g in range(first + 1, len(groups)):
            columns = [spread_lane(groups[g], base + k) for k in range(8)]
            rest = jnp.where(inside, 0.0, groups[g])
            for j in range(8):
                factor = columns[j] * scales[j]
                for k in range(j + 1, 8):
                    columns[k] = columns[k] - factor * heads[j][k - j - 1]
                rest = rest - factor * pivot_rows[j]
            groups[g] = rest
        norm = norms[0]
        for j in range(1, 8):
            norm = jnp.where(row == j, norms[j], norm)
        unit = jnp.where(lane < row + base, own, 0.0)
        result.append(jnp.where(lane == row + base, 1.0, unit) * norm)
    return jnp.concatenate(result, axis=0)


def diagonal(shape, offset):
    row = lax.broadcasted_iota(jnp.int32, shape, 0) + offset
    return row == lax.broadcasted_iota(jnp.int32, shape, 1)


def span(panel, number=1):
    return slice(panel * PANEL, (panel + number) * PANEL)


FIRST, SECOND = slice(0, BLOCK), slice(BLOCK, PANEL)


def panels_kernel(panels, total, inputs, outputs, scratch, here_ref, *refs):
    names = [*inputs, *outputs, *scratch]
    ref = dict(zip(names, refs))
    here = here_ref[0]
    if panels[0] == 0:
        sums = ref["rows", 0][:, CHUNK * PANEL :].astype(f32)
        sums = jnp.sum(sums, axis=0, keepdims=True)
        count, *norms = (sums[:, i : i + 1] for i in range(NOTES, NOTES + 4))
        scale = 2.0 / count
        trace = norms[0] + (norms[1] + norms[2])
        damp = 0.01 * scale * trace / (total * PANEL)
        ref["stats"][...] = jnp.concatenate(
            [jnp.broadcast_to(value, (8, BLOCK)) for value in (scale, damp)], axis=0
        )
    scale, damp = ref["stats"][0:1, 0:1], ref["stats"][8:9, 0:1]
    top, bottom, across, between = (ref[n] for n in ("top", "bottom", "across", "between"))
    turned = ref["turned"]

    def work(panel):
        return ref["work", panel % 2]

    def lower(panel):
        return ref["lower", panel % 2]

    def load(name, panel, rows=slice(None), lanes=slice(None)):
        return [ref[name, panel][i, rows, lanes] for i in range(3)]

    def store(target, rows, lanes, parts):
        for i in range(target.shape[0]):
            target[i, rows, lanes] = parts[i]

    def start(panel):
        chunk, place = divmod(panel, CHUNK)
        turned[...] = ref["rows", chunk][:, span(place)].T
        for c in range(chunk + 1):
            number = CHUNK if c < chunk else place + 1
            gram = multiply(turned[...], ref["rows", c][:, span(0, number)]) * scale
            if c == chunk:
                gram = gram + jnp.where(diagonal(gram.shape, place * PANEL), damp, 0.0)
            work(panel)[:, span(CHUNK * c, number)] = gram

    def solve(panel, sources):
        rows = work(panel)
        for p in sources:
            inverse = right_of(load("solve", p))
            solved = multiply(left_of(pieces(rows[:, span(p)])), inverse)
            parts = pieces(solved)
            store(lower(panel), slice(None), span(p), parts)
            store(ref["upper", panel], span(p), slice(None), pieces(solved.T))
            left = left_of(parts)
            for c in range(p + 1, panel + 1):
                right = right_of(load("upper", c, span(p)))
                rows[:, span(c)] = rows[:, span(c)] - multiply(left, right)

    def solve_half(panel, half, inverse):
        rows, p = work(panel), panel - 1
        lanes = slice(p * PANEL + half * BLOCK, p * PANEL + (half + 1) * BLOCK)
        solved = product(rows[:, lanes], inverse.T)
        flipped = solved.T
        store(lower(panel), slice(None), lanes, pieces(solved))
        store(ref["upper", panel], lanes, slice(None), pieces(flipped))
        if half == 0:
            lanes = slice(p * PANEL + BLOCK, panel * PANEL)
            rows[:, lanes] = rows[:, lanes] - product(solved, across[...])
        rows[:, span(panel)] = rows[:, span(panel)] - product(solved, flipped)

    def block(panel, row, lane):
        lanes = slice(panel * PANEL + lane * BLOCK, panel * PANEL + (lane + 1) * BLOCK)
        return work(panel)[row * BLOCK : (row + 1) * BLOCK, lanes]

    def factor(panel, half):
        value = block(panel, half, half)
        return inverse_factor([value[8 * g : 8 * g + 8, :] for g in range(BLOCK // 8)])

    def inverse_of():
        zero = jnp.zeros((BLOCK, BLOCK), f32)
        corner = -product(bottom[...], between[...])
        return jnp.concatenate(
            [
                jnp.concatenate([top[...], zero], axis=1),
                jnp.concatenate([corner, bottom[...]], axis=1),
            ],
            axis=0,
        )

    def short_sum(panel, sources):
        lanes = slice(sources[0] * PANEL, (sources[-1] + 1) * PANEL)
        high, middle = lower(panel)[0, :, lanes], lower(panel)[1, :, lanes]
        solved_high = [ref["high", p][...] for p in sources]
        solved_middle = [ref["middle", p][...] for p in sources]
        return multiply(
            jnp.concatenate([high, high, middle], axis=1),
            jnp.concatenate([*solved_high, *solved_middle, *solved_high], axis=0),
        )

    def unit(panel):
        return diagonal((PANEL, SHARE * PANEL), (panel - here * SHARE) * PANEL).astype(f32)

    def finish(panel, inverse, wanted):
        left, right = pieces(inverse), pieces(wanted)
        solved = multiply(
            jnp.concatenate([left[0], left[0], left[1]], axis=1),
            jnp.concatenate([right[0], right[1], right[0]], axis=0),
        )
        high, middle, _ = pieces(solved)
        if panel + 1 == total:
            ref["inverse"][span(panel), :] = high
        else:
            ref["high", panel][...] = high
            ref["middle", panel][...] = middle

    def finish_before(panel):
        before = panel - 1
        inverse = inverse_of()
        store(ref["solve", before], slice(None), slice(None), pieces(inverse.T))
        finish(before, inverse, ref["wanted"][...])

    def hessian(chunk):
        gram = multiply(ref["here"][...], ref["rows", chunk][:, span(0, CHUNK)]) * scale
        spread = diagonal(gram.shape, (here * SHARE - chunk * CHUNK) * PANEL)
        ref["hessian"][:, span(CHUNK * chunk, CHUNK)] = gram + jnp.where(spread, damp, 0.0)

    def phase(body):
        pl.when(here >= 0)(body)

    first, last = panels[0], panels[-1]
    ending = last + 1 == total
    if first == 0:
        start(0)
    else:
        work(first)[:, span(first)] = ref["diagonal_in"][...]
        lower(first)[:, :, : first * PANEL] = ref["lower_in"][...]
        top[...], bottom[...], between[...] = (ref["pending_in"][i] for i in range(3))
        ref["wanted"][...] = ref["wanted_in"][...]
    if ending:
        for helper in range(total // SHARE):

            @pl.when(here == helper)
            def _():
                chunk, place = divmod(helper * SHARE, CHUNK)
                ref["here"][...] = ref["rows", chunk][:, span(place, SHARE)].T

    for t in panels:
        after = t + 1

        @phase
        def _():
            if t > first:
                solve_half(t, 1, bottom[...])
            made = factor(t, 0)
            if t:
                finish_before(t)
            if after < total:
                start(after)
                solve(after, range(0, t // 2))
            else:
                hessian(0)
            top[...] = made

        @phase
        def _():
            made_across = product(top[...], block(t, 0, 1))
            across[...] = made_across
            flipped = made_across.T
            spot = (SECOND, slice(t * PANEL + BLOCK, (t + 1) * PANEL))
            work(t)[spot] = work(t)[spot] - product(flipped, made_across)
            made = factor(t, 1)
            between[...] = product(flipped, top[...])
            if after < total:
                solve(after, range(t // 2, t))
                solve_half(after, 0, top[...])
            else:
                hessian(1)
            ref["wanted"][...] = unit(t) - short_sum(t, range(t)) if t else unit(t)
            bottom[...] = made

    if ending:

        @phase
        def _():
            finish(last, inverse_of(), ref["wanted"][...])

        for p in range(last):
            ref["inverse"][span(p), :] = ref["high", p][...]
    else:
        after = last + 1
        solve_half(after, 1, bottom[...])
        ref["diagonal_out"][...] = work(after)[:, span(after)]
        ref["lower_out"][...] = lower(after)[:, :, : after * PANEL]
        for i, value in enumerate((top, bottom, between)):
            ref["pending_out"][i] = value[...]
        ref["wanted_out"][...] = ref["wanted"][...]


def run_panels(panels, total, here, known):
    shape = jax.ShapeDtypeStruct
    first, last = panels[0], panels[-1]
    ending = last + 1 == total
    after = min(last + 1, total - 1)
    count_rows = known["rows", 0].shape[0]
    square = shape((BLOCK, BLOCK), f32)
    columns = SHARE * PANEL
    made = {}
    for t in range(max(first, 1), after + 1) if first == 0 else range(first + 1, after + 1):
        made["upper", t] = shape((3, t * PANEL, PANEL), bf16)
    for t in range(max(first - 1, 0), last):
        made["solve", t] = shape((3, PANEL, PANEL), bf16)
        made["high", t] = shape((PANEL, columns), bf16)
        made["middle", t] = shape((PANEL, columns), bf16)
    scratch = {name: square for name in ("top", "bottom", "across", "between")}
    for i in range(2):
        scratch["work", i] = shape((PANEL, (after + 1) * PANEL), f32)
        scratch["lower", i] = shape((2, PANEL, max(after, 1) * PANEL), bf16)
    scratch["wanted"] = shape((PANEL, columns), f32)
    scratch["turned"] = shape((PANEL, count_rows), bf16)
    if ending:
        outputs = {
            "hessian": shape((columns, total * PANEL), f32),
            "inverse": shape((total * PANEL, columns), bf16),
        }
        scratch.update(made)
        scratch["here"] = shape((columns, count_rows), bf16)
    else:
        outputs = {
            **made,
            "diagonal_out": shape((PANEL, PANEL), f32),
            "lower_out": shape((2, PANEL, after * PANEL), bf16),
            "pending_out": shape((3, BLOCK, BLOCK), f32),
            "wanted_out": shape((PANEL, columns), f32),
        }
    if first == 0:
        outputs["stats"] = shape((16, BLOCK), f32)
    chunks = after // CHUNK + 1
    inputs = {n: a for n, a in known.items() if n[0] != "rows" or n[1] < chunks}
    in_vmem = pl.BlockSpec(memory_space=pltpu.VMEM)
    results = pl.pallas_call(
        functools.partial(panels_kernel, panels, total, list(inputs), list(outputs), list(scratch)),
        out_shape=list(outputs.values()),
        in_specs=[pl.BlockSpec(memory_space=pltpu.SMEM)] + [in_vmem] * len(inputs),
        out_specs=[in_vmem] * len(outputs),
        scratch_shapes=[pltpu.VMEM(a.shape, a.dtype) for a in scratch.values()],
        compiler_params=pltpu.CompilerParams(vmem_limit_bytes=56 * 2**20),
        cost_estimate=pl.CostEstimate(
            flops=14 * 10**9 * len(panels), bytes_accessed=2**23, transcendentals=0
        ),
        name=f"panels{first}to{last}",
    )(here, *inputs.values())
    return dict(zip(outputs, results))


def factor(here, first, second):
    total = 2 * CHUNK
    known = {("rows", 0): first}
    made = run_panels((0, 1, 2), total, here, known)
    for name in ("diagonal", "lower", "pending", "wanted"):
        known[name + "_in"] = made.pop(name + "_out")
    known.update(made)
    known["rows", 1] = second
    made = run_panels((3, 4, 5, 6, 7), total, here, known)
    return made["hessian"], made["inverse"]


def of_group(value):
    number = lax.axis_size("helper")
    blocks = [value]
    for step in range(1, number):
        pairs = [(i, (i + step) % number) for i in range(number)]
        blocks.append(lax.ppermute(value, "helper", pairs))
    return jnp.concatenate(blocks, axis=0)


def local(tokens, routes, chosen):
    slots = chosen.shape[0]
    block = tokens.shape[0]
    half = tokens.shape[1] // 2
    rest = jnp.sum(jnp.square(tokens.astype(f32)), axis=1, keepdims=True)
    notes = [routes.astype(f32), jnp.ones_like(rest)]
    for _ in range(3):
        piece = lax.reduce_precision(rest, 8, 7)
        notes.append(piece)
        rest = rest - piece
    notes = jnp.concatenate(notes, axis=1)
    notes = jnp.pad(notes, ((0, 0), (0, BLOCK - notes.shape[1]))).astype(bf16)
    group = of_group(jnp.concatenate([tokens[:, :half], notes, tokens[:, half:]], axis=1))
    cut = half + BLOCK
    number = group.shape[0]
    group_routes = group[:, half : half + NOTES].astype(jnp.int32).T
    named = jnp.any(group_routes[None, :, :] == chosen[:, None, None], axis=1)
    place = jnp.arange(number, dtype=jnp.int32)
    earlier = (place[:, None] < place[None, :]) & (place[:, None] // block == place[None, :] // block)
    before = jnp.dot(named.astype(bf16), earlier.astype(bf16), preferred_element_type=f32)
    spot = before.astype(jnp.int32) + place // block * MOST
    spots = jnp.arange(number // block * MOST, dtype=jnp.int32)
    picks = named[:, None, :] & (spot[:, None, :] == spots[None, :, None])
    picks = picks.astype(bf16).reshape(slots * spots.shape[0], number)

    def routed(outgoing):
        outgoing = outgoing.reshape(slots, spots.shape[0], -1)
        arrived = lax.all_to_all(outgoing, "expert", split_axis=0, concat_axis=0, tiled=True)
        return arrived.reshape(slots * spots.shape[0], -1)

    first = routed(multiply(picks, group[:, :cut]).astype(bf16))
    second = multiply(picks, group[:, cut:]).astype(bf16)
    first, second = lax.optimization_barrier((first, second))
    second = routed(second)
    here = lax.axis_index("helper").astype(jnp.int32).reshape(1)
    hessian, inverse = factor(here, first, second)
    return (hessian[None], inverse[None])


def solution(mesh):
    placed = (P(("expert", "helper"), None), P(("expert", "helper"), None), P())
    return jax.shard_map(
        local,
        mesh=mesh,
        in_specs=placed,
        out_specs=(P("expert", "helper", None), P("expert", None, "helper")),
        check_vma=False,
    )
```
